512 devices in a mesh: dp: 128 (over y, z, core), feat: 4 (over x).
Axes of the slice: x: 4, y: 8, z: 8, core: 2. Of those that a mesh axis runs over, the one named last changes fastest.
Arguments:
- features: float32 [65536, 1024], P(('dp', 'feat'))
- queries: float32 [512, 1024], P(('dp', 'feat')), may hold values from -6 to 6
- ridge_sixteenths: int32 [1], replicated, may hold values from 4 to 32
- shard_lists: int32 [128, 8], P('dp'), may hold values from 0 to 7, each once within a row
- counts: int32 [128], P('dp'), may hold values from 2 to 8, as said below
Outputs:
- scores: float32 [512, 8, 4, 2048], P('dp', None, 'feat')
The draws below stay inside these ranges and needn't reach their ends.
Inputs may be any that keep to these rules, and one draw needn't show every extreme that they name: Query block b is scored against the first counts[b] shards of its row of shard_lists; some block has 8 and some has 2. `shard_lists`: each row names every training shard once.
All inputs are finite; a program needn't handle non-finite values.
Results may differ from the reference program's by a relative error of at most 0.0003.
Values sent between devices are 32-bit elements; how exact they have to be, the bound alone decides.
No kernel may reach another device: no remote copies, remote signals or barrier semaphores. Data moves between devices by JAX's collectives and lax.ppermute only.
A program may use at most 64 MiB of HBM per device.

```python
import math
import jax
import jax.numpy as jnp
from jax import lax

K = 1024
ROWS_DEV = 128
QB = 4
NSHARD = 8
GROUP = 16
N_TRAIN = 65536
QUERY_TOTAL = 512
SHARD_COLS = 2048
N_DP = 128
N_FEAT = 4


def draw_features(key, part):
    key = jax.random.fold_in(key, 11)
    keys = jax.random.split(key, 5)
    noise = jax.random.normal(keys[0], (N_TRAIN, K), jnp.float32)
    row_scale = 0.3 * jnp.exp(jax.random.uniform(keys[1], (N_TRAIN, 1), jnp.float32, 0.0, math.log(10.0)))
    mixed = noise + 0.6 * jnp.roll(noise, 1, axis=1) + 0.5 * jnp.roll(noise, 5, axis=1) - 0.4 * jnp.roll(noise, 37, axis=1)
    loading = jax.random.normal(keys[2], (N_TRAIN, 1), jnp.float32)
    direction = jax.random.normal(keys[3], (K,), jnp.float32)
    mixed = mixed + 0.7 * loading * direction
    column_scale = 0.3 * jnp.exp(jax.random.uniform(keys[4], (K,), jnp.float32, 0.0, math.log(10.0)))
    return mixed * column_scale * row_scale


def draw_counts(key, part):
    key = jax.random.fold_in(key, 12)
    keys = jax.random.split(key, 3)
    values = jax.random.randint(keys[0], (N_DP,), 2, NSHARD + 1)
    first = jax.random.randint(keys[1], (), 0, N_DP)
    second = (first + 1 + jax.random.randint(keys[2], (), 0, N_DP - 1)) % N_DP
    values = values.at[first].set(NSHARD)
    values = values.at[second].set(2)
    return values.astype(jnp.int32)


def block_scale(own_key, dims, pieces, low, largest):
    factor_of, own = 1.0, jax.random.fold_in(own_key, 6)
    for dim, shards_of in pieces:
        draws = jnp.exp(jax.random.uniform(jax.random.fold_in(own, dim), (shards_of,), jnp.float32, low / len(pieces), largest / len(pieces)))
        factor_of = factor_of * jnp.repeat(draws, dims[dim] // shards_of).reshape([-1 if axis == dim else 1 for axis in range(len(dims))])
    return factor_of


def normal_values(key, shape, width, limit, shards=(), kind=jnp.bfloat16):
    drawn = jax.random.normal(key, shape, jnp.float32) * width
    if len(shards) > 0:
        drawn = block_scale(key, shape, shards, -0.22, 0.18) * drawn
    return jnp.clip(drawn, min=-limit, max=limit).astype(kind)


def setup_inputs(seed: int = 0) -> dict:
    arg_keys = jax.random.split(jax.random.key(seed), 6)
    features = draw_features(jax.random.fold_in(arg_keys[5], 71), 0)
    queries = normal_values(arg_keys[1], (QUERY_TOTAL, K), 1.0, 6.0, ((0, 512),), jnp.float32)
    ridge_sixteenths = jax.random.randint(arg_keys[2], (1,), 4, 33).astype(jnp.int32)
    shard_lists = jax.vmap(lambda own: jax.random.permutation(own, NSHARD))(jax.random.split(arg_keys[3], N_DP)).reshape((N_DP, NSHARD)).astype(jnp.int32)
    counts = draw_counts(jax.random.fold_in(arg_keys[5], 71), 0)
    return {"features": features, "queries": queries, "ridge_sixteenths": ridge_sixteenths, "shard_lists": shard_lists, "counts": counts}


TOP_PRECISION = lax.Precision.HIGHEST

def whiten(gram_matrix, query_rows):
    factor = jnp.linalg.cholesky(gram_matrix)
    halfway = jax.scipy.linalg.solve_triangular(factor, query_rows.T, lower=True)
    solved = jax.scipy.linalg.solve_triangular(factor, halfway, lower=True, trans=1)
    return solved.T

def reference(features, queries, ridge_sixteenths, shard_lists, counts):
    ridge_weight = ridge_sixteenths[0].astype(jnp.float32) / 16.0
    gram_matrix = jnp.dot(features.T.astype(jnp.float32), features.astype(jnp.float32), precision=TOP_PRECISION, preferred_element_type=jnp.float32) / N_TRAIN
    gram_matrix = gram_matrix + ridge_weight * jnp.eye(K, dtype=jnp.float32)
    whitened = whiten(gram_matrix, queries)
    attribution_scale = 1.0 / math.sqrt(K)
    grouped = features.reshape(NSHARD, GROUP, N_FEAT, ROWS_DEV, K)
    slot_ids = jnp.arange(NSHARD, dtype=jnp.int32)

    def per_block(block_items):
        block_rows, listing, live_count = block_items

        def per_slot(slot_index):
            shard_rows = lax.dynamic_index_in_dim(grouped, listing[slot_index], 0, keepdims=False)
            partial_scores = jnp.einsum('qk,gfrk->qfgr', block_rows, shard_rows, precision=TOP_PRECISION) * attribution_scale
            partial_scores = partial_scores.reshape(QB, N_FEAT, GROUP * ROWS_DEV)
            return jnp.where(slot_index < live_count, partial_scores, jnp.zeros_like(partial_scores))
        return lax.map(per_slot, slot_ids)
    score_table = lax.map(per_block, (whitened.reshape(N_DP, QB, K), shard_lists, counts))
    return score_table.transpose(0, 2, 1, 3, 4).reshape(QUERY_TOTAL, NSHARD, N_FEAT, SHARD_COLS)
```

```python
import math

import jax
import jax.numpy as jnp
from jax import lax
from jax.experimental import pallas as pl
from jax.experimental.pallas import tpu as pltpu
from jax.sharding import Mesh
from jax.sharding import PartitionSpec as P

NSHARD = 8
T = 128
TOP_PRECISION = lax.Precision.HIGHEST
GRID = ("y", "z")
ALL = ("y", "z", "core", "x")


def dot(a, b, over_a, over_b):
    return lax.dot_general(
        a,
        b,
        (((over_a,), (over_b,)), ((), ())),
        precision=TOP_PRECISION,
        preferred_element_type=jnp.float32,
    )


def place(n, i, j):
    return (i * n - i * (i - 1) // 2 + j - i) * T


def gram_kernel(f_ref, g_ref):
    n = f_ref.shape[1] // T
    for i in range(n):
        row = dot(f_ref[:, i * T : (i + 1) * T], f_ref[:, i * T :], 0, 0)
        for j in range(i, n):
            g_ref[pl.ds(place(n, i, j), T), :] = row[:, (j - i) * T : (j - i + 1) * T]


def spread(row):
    return jnp.broadcast_to(row, (8, T))


def factor_block(rows, lane, sub):
    rows = list(rows)
    count = len(rows)
    lower, scaled = [], []
    for b in range(count):
        base = 8 * b
        columns = [spread(rows[b][:, base + j : base + j + 1]) for j in range(8)]
        inside = (lane >= base) & (lane < base + 8)
        work = jnp.where(inside, (lane - base == sub).astype(jnp.float32), rows[b])
        lower.append(jnp.where(lane < base + 8, work, 0.0))
        for j in range(8):
            inverse = 1.0 / columns[j][j : j + 1, :]
            pivot = sub == j
            row = spread(work[j : j + 1, :] * inverse)
            work = jnp.where(pivot, row, work - columns[j] * row)
            for l in range(j + 1, 8):
                entry = spread(columns[l][j : j + 1, :] * inverse)
                columns[l] = jnp.where(pivot, entry, columns[l] - columns[j] * entry)
        scaled.append(jnp.where(lane < base + 8, work, 0.0))
        pivots = [spread(work[j : j + 1, :]) for j in range(8)]
        for i in range(b + 1, count):
            terms = [spread(rows[i][:, base + j : base + j + 1]) * pivots[j] for j in range(8)]
            while len(terms) > 1:
                terms = [terms[p] + terms[p + 1] for p in range(0, len(terms), 2)]
            rows[i] = jnp.where(inside, 0.0, rows[i]) - terms[0]
    return lower, scaled


def solve_kernel(total_rows, ridge_ref, core_ref, mine_ref, other_ref, f_ref, y_ref, a, x, pb, nm):
    n = f_ref.shape[1] // T
    half = mine_ref.shape[0]
    lane = lax.broadcasted_iota(jnp.int32, (8, T), 1)
    sub = lax.broadcasted_iota(jnp.int32, (8, T), 0)
    ridge = ridge_ref[0].astype(jnp.float32) / 16.0
    core = core_ref[0]
    a[pl.ds(pl.multiple_of(core * half, T), half), :] = mine_ref[...] * (1.0 / total_rows)
    a[pl.ds(pl.multiple_of((1 - core) * half, T), half), :] = other_ref[...] * (1.0 / total_rows)
    x[...] = f_ref[...]
    for k in range(n):
        start = place(n, k, k)
        rows = [
            a[pl.ds(start + 8 * i, 8), :] + jnp.where(lane - 8 * i == sub, ridge, 0.0)
            for i in range(T // 8)
        ]
        lower, scaled = factor_block(rows, lane, sub)
        for i in range(T // 8):
            nm[pl.ds(k * 2 * T + 8 * i, 8), :] = lower[i]
            nm[pl.ds(k * 2 * T + T + 8 * i, 8), :] = scaled[i]
        both = nm[pl.ds(k * 2 * T, 2 * T), :]
        fz = dot(x[:, k * T : (k + 1) * T], both, 1, 1)
        y_ref[:, k * T : (k + 1) * T] = fz[:, T:]
        for j in range(k + 1, n):
            panel = dot(both, a[pl.ds(place(n, k, j), T), :], 1, 0)
            a[pl.ds(place(n, k, j), T), :] = panel[:T]
            pb[pl.ds(place(n, k, j), T), :] = panel[T:]
        for i in range(k + 1, n):
            left = a[pl.ds(place(n, k, i), T), :]
            for j in range(i, n):
                a[pl.ds(place(n, i, j), T), :] -= dot(left, pb[pl.ds(place(n, k, j), T), :], 0, 0)
            x[:, i * T : (i + 1) * T] -= dot(fz[:, :T], pb[pl.ds(place(n, k, i), T), :], 1, 0)
    for k in reversed(range(n)):
        yk = dot(y_ref[:, k * T : (k + 1) * T], nm[pl.ds(k * 2 * T, T), :], 1, 0)
        y_ref[:, k * T : (k + 1) * T] = yk
        for i in range(k):
            y_ref[:, i * T : (i + 1) * T] -= dot(yk, pb[pl.ds(place(n, i, k), T), :], 1, 1)


def pick_kernel(listing_ref, count_ref, got_ref, out_ref):
    group = got_ref.shape[1]
    for l in range(NSHARD):
        live = l < count_ref[0]
        shard = listing_ref[0, l]
        for g in range(group):
            out_ref[:, l, g * T : (g + 1) * T] = jnp.where(live, got_ref[shard, g], 0.0)


def shards(features, queries, ridge_sixteenths, shard_lists, counts):
    width = features.shape[1]
    n = width // T
    n_y, n_z, n_x = lax.axis_size("y"), lax.axis_size("z"), lax.axis_size("x")
    n_grid = n_y * n_z
    total_rows = features.shape[0] * n_grid * 2 * n_x
    packed = n * (n + 1) // 2 * T
    half = packed // 2
    piece = half // n_x
    chunk = piece * T // n_grid
    core = lax.axis_index("core")
    vmem = pl.BlockSpec(memory_space=pltpu.VMEM)
    smem = pl.BlockSpec(memory_space=pltpu.SMEM)
    swap = [(0, 1), (1, 0)]

    all_queries = lax.all_gather(queries, ALL, axis=0, tiled=True)
    with jax.named_scope("gram"):
        gram = pl.pallas_call(
            gram_kernel,
            out_shape=jax.ShapeDtypeStruct((packed, T), jnp.float32),
            in_specs=[vmem],
            out_specs=vmem,
            compiler_params=pltpu.CompilerParams(vmem_limit_bytes=32 * 1024 * 1024),
        )(features)
    with jax.named_scope("scatter"):
        keep = lax.dynamic_slice_in_dim(gram, core * half, half, 0)
        give = lax.dynamic_slice_in_dim(gram, (1 - core) * half, half, 0)
        part = keep + lax.ppermute(give, "core", swap)
        part = lax.all_to_all(part.reshape(n_x, piece, T), "x", 0, 0, tiled=True).sum(0)
        part = lax.all_to_all(part.reshape(n_grid, chunk), GRID, 0, 0, tiled=True).sum(0)
    with jax.named_scope("gather"):
        part = lax.all_to_all(jnp.broadcast_to(part[None], (n_grid, chunk)), GRID, 0, 0, tiled=True)
        part = jnp.broadcast_to(part.reshape(1, piece, T), (n_x, piece, T))
        mine = lax.all_to_all(part, "x", 0, 0, tiled=True).reshape(half, T)
        other = lax.ppermute(mine, "core", swap)
    with jax.named_scope("solve"):
        solved = pl.pallas_call(
            lambda *refs: solve_kernel(total_rows, *refs),
            out_shape=jax.ShapeDtypeStruct(features.shape, jnp.float32),
            in_specs=[smem, smem, vmem, vmem, vmem],
            out_specs=vmem,
            scratch_shapes=[
                pltpu.VMEM((packed, T), jnp.float32),
                pltpu.VMEM(features.shape, jnp.float32),
                pltpu.VMEM((packed, T), jnp.float32),
                pltpu.VMEM((2 * width, T), jnp.float32),
            ],
            compiler_params=pltpu.CompilerParams(vmem_limit_bytes=40 * 1024 * 1024),
        )(ridge_sixteenths, core.reshape(1).astype(jnp.int32), mine, other, features)
    with jax.named_scope("scores"):
        table = dot(all_queries, solved, 1, 1) * (1.0 / math.sqrt(width))
    n_dp = n_grid * 2
    block = table.shape[0] // n_dp
    group = n_dp // NSHARD
    got = lax.all_to_all(table.reshape(n_dp, block, T), ("y", "z", "core"), 0, 0, tiled=True)
    with jax.named_scope("pick"):
        picked = pl.pallas_call(
            pick_kernel,
            out_shape=jax.ShapeDtypeStruct((block, NSHARD, group * T), jnp.float32),
            in_specs=[smem, smem, vmem],
            out_specs=vmem,
        )(shard_lists, counts, got.reshape(NSHARD, group, block, T))
    return picked.reshape(block, NSHARD, 1, group * T)


def solution(mesh):
    n_dp, n_x = mesh.devices.shape
    side = math.isqrt(n_dp // 2)
    chips = Mesh(mesh.devices.reshape(side, side, 2, n_x), ALL)
    dp = ("y", "z", "core")
    placed = (P(ALL, None), P(ALL, None), P(), P(dp, None), P(dp))
    return jax.shard_map(
        shards, mesh=chips, in_specs=placed, out_specs=P(dp, None, "x", None), check_vma=False
    )
```

```python
import math

import jax
import jax.numpy as jnp
from jax import lax
from jax.experimental import pallas as pl
from jax.experimental.pallas import tpu as pltpu
from jax.sharding import Mesh
from jax.sharding import PartitionSpec as P

NSHARD = 8
T = 128
TOP_PRECISION = lax.Precision.HIGHEST
GRID = ("y", "z")
ALL = ("y", "z", "core", "x")


def dot(a, b, over_a, over_b):
    return lax.dot_general(
        a,
        b,
        (((over_a,), (over_b,)), ((), ())),
        precision=TOP_PRECISION,
        preferred_element_type=jnp.float32,
    )


def parts_of(v):
    high = v.astype(jnp.bfloat16)
    rest = v - high.astype(jnp.float32)
    middle = rest.astype(jnp.bfloat16)
    return high, middle, (rest - middle.astype(jnp.float32)).astype(jnp.bfloat16)


def long_dot(a, b, over_a, over_b):
    a1, a2, a3 = parts_of(a)
    b1, b2, b3 = parts_of(b)
    return lax.dot_general(
        jnp.concatenate([a1, a2, a1, a2, a1, a3], axis=over_a),
        jnp.concatenate([b1, b1, b2, b2, b3, b1], axis=over_b),
        (((over_a,), (over_b,)), ((), ())),
        preferred_element_type=jnp.float32,
    )


def place(n, i, j):
    return (i * n - i * (i - 1) // 2 + j - i) * T


def gram_kernel(f_ref, g_ref):
    n = f_ref.shape[1] // T
    for i in range(n):
        row = dot(f_ref[:, i * T : (i + 1) * T], f_ref[:, i * T :], 0, 0)
        for j in range(i, n):
            g_ref[pl.ds(place(n, i, j), T), :] = row[:, (j - i) * T : (j - i + 1) * T]


def spread(row):
    return jnp.broadcast_to(row, (8, T))


def factor_block(rows, lane, sub, give):
    rows = list(rows)
    count = len(rows)
    for b in range(count):
        base = 8 * b
        columns = [spread(rows[b][:, base + j : base + j + 1]) for j in range(8)]
        inside = (lane >= base) & (lane < base + 8)
        work = jnp.where(inside, (lane - base == sub).astype(jnp.float32), rows[b])
        lower = jnp.where(lane < base + 8, work, 0.0)
        for j in range(8):
            inverse = 1.0 / columns[j][j : j + 1, :]
            pivot = sub == j
            row = spread(work[j : j + 1, :] * inverse)
            work = jnp.where(pivot, row, work - columns[j] * row)
            for l in range(j + 1, 8):
                entry = spread(columns[l][j : j + 1, :] * inverse)
                columns[l] = jnp.where(pivot, entry, columns[l] - columns[j] * entry)
        give(b, lower, jnp.where(lane < base + 8, work, 0.0))
        pivots = [spread(work[j : j + 1, :]) for j in range(8)]
        for i in range(b + 1, count):
            terms = [spread(rows[i][:, base + j : base + j + 1]) * pivots[j] for j in range(8)]
            while len(terms) > 1:
                terms = [terms[p] + terms[p + 1] for p in range(0, len(terms), 2)]
            rows[i] = jnp.where(inside, 0.0, rows[i]) - terms[0]
        yield b


def solve_kernel(total_rows, ridge_ref, core_ref, mine_ref, other_ref, f_ref, y_ref, a, x, pb, nm):
    n = f_ref.shape[1] // T
    half = mine_ref.shape[0]
    lane = lax.broadcasted_iota(jnp.int32, (8, T), 1)
    sub = lax.broadcasted_iota(jnp.int32, (8, T), 0)
    ridge = ridge_ref[0].astype(jnp.float32) / 16.0
    core = core_ref[0]
    a[pl.ds(pl.multiple_of(core * half, T), half), :] = mine_ref[...] * (1.0 / total_rows)
    a[pl.ds(pl.multiple_of((1 - core) * half, T), half), :] = other_ref[...] * (1.0 / total_rows)
    x[...] = f_ref[...]

    def block(i, j):
        return pl.ds(place(n, i, j), T)

    def panel(k, j):
        both = long_dot(nm[pl.ds(k * 2 * T, 2 * T), :], a[block(k, j), :], 1, 0)
        a[block(k, j), :] = both[:T]
        pb[block(k, j), :] = both[T:]

    def update(k, i, j):
        a[block(i, j), :] -= long_dot(a[block(k, i), :], pb[block(k, j), :], 0, 0)

    def forward(k):
        both = long_dot(x[:, k * T : (k + 1) * T], nm[pl.ds(k * 2 * T, 2 * T), :], 1, 1)
        x[:, k * T : (k + 1) * T] = both[:, :T]
        y_ref[:, k * T : (k + 1) * T] = both[:, T:]

    def forward_update(k, i):
        x[:, i * T : (i + 1) * T] -= long_dot(x[:, k * T : (k + 1) * T], pb[block(k, i), :], 1, 0)

    waiting = []
    for k in range(n):
        start = place(n, k, k)
        rows = [
            a[pl.ds(start + 8 * i, 8), :] + jnp.where(lane - 8 * i == sub, ridge, 0.0)
            for i in range(T // 8)
        ]

        def give(b, lower, scaled):
            nm[pl.ds(k * 2 * T + 8 * b, 8), :] = lower
            nm[pl.ds(k * 2 * T + T + 8 * b, 8), :] = scaled

        total, done = len(waiting), 0
        for b in factor_block(rows, lane, sub, give):
            while waiting and done < -(-total * (b + 1) // 14):
                step, *where = waiting.pop(0)
                step(*where)
                done += 1
        if k + 1 < n:
            panel(k, k + 1)
            update(k, k + 1, k + 1)
            waiting = [(panel, k, j) for j in range(k + 2, n)] + [(forward, k)]
            for i in range(k + 1, n):
                waiting += [(update, k, i, j) for j in range(i, n) if j > k + 1]
                waiting += [(forward_update, k, i)]
    forward(n - 1)
    for k in reversed(range(n)):
        yk = long_dot(y_ref[:, k * T : (k + 1) * T], nm[pl.ds(k * 2 * T, T), :], 1, 0)
        y_ref[:, k * T : (k + 1) * T] = yk
        for i in reversed(range(k)):
            y_ref[:, i * T : (i + 1) * T] -= long_dot(yk, pb[block(i, k), :], 1, 1)


def pick_kernel(listing_ref, count_ref, got_ref, out_ref):
    group = got_ref.shape[1]
    for l in range(NSHARD):
        live = l < count_ref[0]
        shard = listing_ref[0, l]
        for g in range(group):
            tile = jnp.where(live, got_ref[shard, g], 0.0)
            for q in range(got_ref.shape[2]):
                out_ref[q, l, :, g * T : (g + 1) * T] = tile[q : q + 1]


def shards(features, queries, ridge_sixteenths, shard_lists, counts):
    width = features.shape[1]
    n = width // T
    n_y, n_z, n_x = lax.axis_size("y"), lax.axis_size("z"), lax.axis_size("x")
    n_grid = n_y * n_z
    total_rows = features.shape[0] * n_grid * 2 * n_x
    packed = n * (n + 1) // 2 * T
    half = packed // 2
    piece = half // n_x
    chunk = piece * T // n_grid
    core = lax.axis_index("core")
    vmem = pl.BlockSpec(memory_space=pltpu.VMEM)
    smem = pl.BlockSpec(memory_space=pltpu.SMEM)
    swap = [(0, 1), (1, 0)]

    all_queries = lax.all_gather(queries, ALL, axis=0, tiled=True)
    with jax.named_scope("gram"):
        gram = pl.pallas_call(
            gram_kernel,
            out_shape=jax.ShapeDtypeStruct((packed, T), jnp.float32),
            in_specs=[vmem],
            out_specs=vmem,
            compiler_params=pltpu.CompilerParams(vmem_limit_bytes=32 * 1024 * 1024),
        )(features)
    with jax.named_scope("scatter"):
        keep = lax.dynamic_slice_in_dim(gram, core * half, half, 0)
        give = lax.dynamic_slice_in_dim(gram, (1 - core) * half, half, 0)
        part = keep + lax.ppermute(give, "core", swap)
        part = lax.all_to_all(part.reshape(n_x, piece, T), "x", 0, 0, tiled=True).sum(0)
        part = lax.all_to_all(part.reshape(n_grid, chunk), GRID, 0, 0, tiled=True).sum(0)
    with jax.named_scope("gather"):
        part = lax.all_to_all(jnp.broadcast_to(part[None], (n_grid, chunk)), GRID, 0, 0, tiled=True)
        part = jnp.broadcast_to(part.reshape(1, piece, T), (n_x, piece, T))
        mine = lax.all_to_all(part, "x", 0, 0, tiled=True).reshape(half, T)
        other = lax.ppermute(mine, "core", swap)
    with jax.named_scope("solve"):
        solved = pl.pallas_call(
            lambda *refs: solve_kernel(total_rows, *refs),
            out_shape=jax.ShapeDtypeStruct(features.shape, jnp.float32),
            in_specs=[smem, smem, vmem, vmem, vmem],
            out_specs=vmem,
            scratch_shapes=[
                pltpu.VMEM((packed, T), jnp.float32),
                pltpu.VMEM(features.shape, jnp.float32),
                pltpu.VMEM((packed, T), jnp.float32),
                pltpu.VMEM((2 * width, T), jnp.float32),
            ],
            compiler_params=pltpu.CompilerParams(vmem_limit_bytes=40 * 1024 * 1024),
        )(ridge_sixteenths, core.reshape(1).astype(jnp.int32), mine, other, features)
    with jax.named_scope("scores"):
        table = dot(all_queries, solved, 1, 1) * (1.0 / math.sqrt(width))
    n_dp = n_grid * 2
    block = table.shape[0] // n_dp
    group = n_dp // NSHARD
    got = lax.all_to_all(table.reshape(n_dp, block, T), ("y", "z", "core"), 0, 0, tiled=True)
    with jax.named_scope("pick"):
        picked = pl.pallas_call(
            pick_kernel,
            out_shape=jax.ShapeDtypeStruct((block, NSHARD, 1, group * T), jnp.float32),
            in_specs=[smem, smem, vmem],
            out_specs=vmem,
        )(shard_lists, counts, got.reshape(NSHARD, group, block, T))
    return picked


def solution(mesh):
    n_dp, n_x = mesh.devices.shape
    side = math.isqrt(n_dp // 2)
    chips = Mesh(mesh.devices.reshape(side, side, 2, n_x), ALL)
    dp = ("y", "z", "core")
    placed = (P(ALL, None), P(ALL, None), P(), P(dp, None), P(dp))
    return jax.shard_map(
        shards, mesh=chips, in_specs=placed, out_specs=P(dp, None, "x", None), check_vma=False
    )
```

```python
import math

import jax
import jax.numpy as jnp
from jax import lax
from jax.experimental import pallas as pl
from jax.experimental.pallas import tpu as pltpu
from jax.sharding import Mesh
from jax.sharding import PartitionSpec as P

NSHARD = 8
T = 128
TOP_PRECISION = lax.Precision.HIGHEST
GRID = ("y", "z")
ALL = ("y", "z", "core", "x")


def dot(a, b, over_a, over_b):
    return lax.dot_general(
        a,
        b,
        (((over_a,), (over_b,)), ((), ())),
        precision=TOP_PRECISION,
        preferred_element_type=jnp.float32,
    )


def parts_of(v):
    high = v.astype(jnp.bfloat16)
    rest = v - high.astype(jnp.float32)
    middle = rest.astype(jnp.bfloat16)
    return high, middle, (rest - middle.astype(jnp.float32)).astype(jnp.bfloat16)


def long_dot(a, b, over_a, over_b):
    a1, a2, a3 = parts_of(a)
    b1, b2, b3 = parts_of(b)
    return lax.dot_general(
        jnp.concatenate([a1, a2, a1, a2, a1, a3], axis=over_a),
        jnp.concatenate([b1, b1, b2, b2, b3, b1], axis=over_b),
        (((over_a,), (over_b,)), ((), ())),
        preferred_element_type=jnp.float32,
    )


def place(n, i, j):
    return (i * n - i * (i - 1) // 2 + j - i) * T


def gram_kernel(core_ref, mine_ref, other_ref, g_ref, rows):
    n = mine_ref.shape[1] // T
    half = g_ref.shape[0] // T
    count = mine_ref.shape[0]
    rows[:count, :] = mine_ref[...]
    rows[count:, :] = other_ref[...]
    for side in range(2):

        @pl.when(core_ref[0] == side)
        def _(side=side):
            for i in range(n):
                first = place(n, i, i) // T
                low, high = max(first, side * half), min(first + n - i, (side + 1) * half)
                if low < high:
                    left = rows[:, i * T : (i + 1) * T]
                    right = rows[:, (i + low - first) * T : (i + high - first) * T]
                    product = dot(left, right, 0, 0)
                    for t in range(high - low):
                        at = pl.ds((low + t - side * half) * T, T)
                        g_ref[at, :] = product[:, t * T : (t + 1) * T]


def spread(row):
    return jnp.broadcast_to(row, (8, T))


def factor_block(rows, lane, sub, give):
    rows = list(rows)
    count = len(rows)
    for b in range(count):
        base = 8 * b
        columns = [spread(rows[b][:, base + j : base + j + 1]) for j in range(8)]
        inside = (lane >= base) & (lane < base + 8)
        work = jnp.where(inside, (lane - base == sub).astype(jnp.float32), rows[b])
        lower = jnp.where(lane < base + 8, work, 0.0)
        for j in range(8):
            inverse = 1.0 / columns[j][j : j + 1, :]
            pivot = sub == j
            row = spread(work[j : j + 1, :] * inverse)
            work = jnp.where(pivot, row, work - columns[j] * row)
            for l in range(j + 1, 8):
                entry = spread(columns[l][j : j + 1, :] * inverse)
                columns[l] = jnp.where(pivot, entry, columns[l] - columns[j] * entry)
        give(b, lower, jnp.where(lane < base + 8, work, 0.0))
        pivots = [spread(work[j : j + 1, :]) for j in range(8)]
        for i in range(b + 1, count):
            terms = [spread(rows[i][:, base + j : base + j + 1]) * pivots[j] for j in range(8)]
            while len(terms) > 1:
                terms = [terms[p] + terms[p + 1] for p in range(0, len(terms), 2)]
            rows[i] = jnp.where(inside, 0.0, rows[i]) - terms[0]
        yield b


def solve_kernel(total_rows, ridge_ref, core_ref, mine_ref, other_ref, f_ref, y_ref, a, x, pb, nm):
    n = f_ref.shape[1] // T
    half = mine_ref.shape[0]
    lane = lax.broadcasted_iota(jnp.int32, (8, T), 1)
    sub = lax.broadcasted_iota(jnp.int32, (8, T), 0)
    ridge = ridge_ref[0].astype(jnp.float32) / 16.0
    core = core_ref[0]
    a[pl.ds(pl.multiple_of(core * half, T), half), :] = mine_ref[...] * (1.0 / total_rows)
    a[pl.ds(pl.multiple_of((1 - core) * half, T), half), :] = other_ref[...] * (1.0 / total_rows)
    x[...] = f_ref[...]

    def block(i, j):
        return pl.ds(place(n, i, j), T)

    def panel(k, j):
        both = long_dot(nm[pl.ds(k * 2 * T, 2 * T), :], a[block(k, j), :], 1, 0)
        a[block(k, j), :] = both[:T]
        pb[block(k, j), :] = both[T:]

    def update(k, i, j):
        a[block(i, j), :] -= long_dot(a[block(k, i), :], pb[block(k, j), :], 0, 0)

    def forward(k):
        both = long_dot(x[:, k * T : (k + 1) * T], nm[pl.ds(k * 2 * T, 2 * T), :], 1, 1)
        x[:, k * T : (k + 1) * T] = both[:, :T]
        y_ref[:, k * T : (k + 1) * T] = both[:, T:]

    def forward_update(k, i):
        x[:, i * T : (i + 1) * T] -= long_dot(x[:, k * T : (k + 1) * T], pb[block(k, i), :], 1, 0)

    waiting = []
    for k in range(n):
        start = place(n, k, k)
        rows = [
            a[pl.ds(start + 8 * i, 8), :] + jnp.where(lane - 8 * i == sub, ridge, 0.0)
            for i in range(T // 8)
        ]

        def give(b, lower, scaled):
            nm[pl.ds(k * 2 * T + 8 * b, 8), :] = lower
            nm[pl.ds(k * 2 * T + T + 8 * b, 8), :] = scaled

        total, done = len(waiting), 0
        for b in factor_block(rows, lane, sub, give):
            while waiting and done < -(-total * (b + 1) // 14):
                step, *where = waiting.pop(0)
                step(*where)
                done += 1
        if k + 1 < n:
            panel(k, k + 1)
            update(k, k + 1, k + 1)
            waiting = [(panel, k, j) for j in range(k + 2, n)] + [(forward, k)]
            for i in range(k + 1, n):
                waiting += [(update, k, i, j) for j in range(i, n) if j > k + 1]
                waiting += [(forward_update, k, i)]
    forward(n - 1)
    for k in reversed(range(n)):
        yk = long_dot(y_ref[:, k * T : (k + 1) * T], nm[pl.ds(k * 2 * T, T), :], 1, 0)
        y_ref[:, k * T : (k + 1) * T] = yk
        for i in reversed(range(k)):
            y_ref[:, i * T : (i + 1) * T] -= long_dot(yk, pb[block(i, k), :], 1, 1)


def pick_kernel(listing_ref, count_ref, got_ref, out_ref):
    group = got_ref.shape[1]
    for l in range(NSHARD):
        live = l < count_ref[0]
        shard = listing_ref[0, l]
        for g in range(group):
            tile = jnp.where(live, got_ref[shard, g], 0.0)
            for q in range(got_ref.shape[2]):
                out_ref[q, l, :, g * T : (g + 1) * T] = tile[q : q + 1]


def shards(features, queries, ridge_sixteenths, shard_lists, counts):
    width = features.shape[1]
    n = width // T
    n_y, n_z, n_x = lax.axis_size("y"), lax.axis_size("z"), lax.axis_size("x")
    n_grid = n_y * n_z
    total_rows = features.shape[0] * n_grid * 2 * n_x
    packed = n * (n + 1) // 2 * T
    half = packed // 2
    piece = half // n_x
    chunk = piece * T // n_grid
    core = lax.axis_index("core")
    vmem = pl.BlockSpec(memory_space=pltpu.VMEM)
    smem = pl.BlockSpec(memory_space=pltpu.SMEM)
    swap = [(0, 1), (1, 0)]

    all_queries = lax.all_gather(queries, ALL, axis=0, tiled=True)
    core_here = core.reshape(1).astype(jnp.int32)
    with jax.named_scope("gram"):
        neighbour = lax.ppermute(features, "core", swap)
        part = pl.pallas_call(
            gram_kernel,
            out_shape=jax.ShapeDtypeStruct((half, T), jnp.float32),
            in_specs=[smem, vmem, vmem],
            out_specs=vmem,
            scratch_shapes=[pltpu.VMEM((2 * features.shape[0], width), jnp.float32)],
            compiler_params=pltpu.CompilerParams(vmem_limit_bytes=32 * 1024 * 1024),
        )(core_here, features, neighbour)
    with jax.named_scope("scatter"):
        part = lax.all_to_all(part.reshape(n_x, piece, T), "x", 0, 0, tiled=True).sum(0)
        part = lax.all_to_all(part.reshape(n_grid, chunk), GRID, 0, 0, tiled=True).sum(0)
    with jax.named_scope("gather"):
        part = lax.all_to_all(jnp.broadcast_to(part[None], (n_grid, chunk)), GRID, 0, 0, tiled=True)
        part = jnp.broadcast_to(part.reshape(1, piece, T), (n_x, piece, T))
        mine = lax.all_to_all(part, "x", 0, 0, tiled=True).reshape(half, T)
        other = lax.ppermute(mine, "core", swap)
    with jax.named_scope("solve"):
        solved = pl.pallas_call(
            lambda *refs: solve_kernel(total_rows, *refs),
            out_shape=jax.ShapeDtypeStruct(features.shape, jnp.float32),
            in_specs=[smem, smem, vmem, vmem, vmem],
            out_specs=vmem,
            scratch_shapes=[
                pltpu.VMEM((packed, T), jnp.float32),
                pltpu.VMEM(features.shape, jnp.float32),
                pltpu.VMEM((packed, T), jnp.float32),
                pltpu.VMEM((2 * width, T), jnp.float32),
            ],
            compiler_params=pltpu.CompilerParams(vmem_limit_bytes=40 * 1024 * 1024),
        )(ridge_sixteenths, core_here, mine, other, features)
    with jax.named_scope("scores"):
        table = dot(all_queries, solved, 1, 1) * (1.0 / math.sqrt(width))
    n_dp = n_grid * 2
    block = table.shape[0] // n_dp
    group = n_dp // NSHARD
    got = lax.all_to_all(table.reshape(n_dp, block, T), ("y", "z", "core"), 0, 0, tiled=True)
    with jax.named_scope("pick"):
        picked = pl.pallas_call(
            pick_kernel,
            out_shape=jax.ShapeDtypeStruct((block, NSHARD, 1, group * T), jnp.float32),
            in_specs=[smem, smem, vmem],
            out_specs=vmem,
        )(shard_lists, counts, got.reshape(NSHARD, group, block, T))
    return picked


def solution(mesh):
    n_dp, n_x = mesh.devices.shape
    side = math.isqrt(n_dp // 2)
    chips = Mesh(mesh.devices.reshape(side, side, 2, n_x), ALL)
    dp = ("y", "z", "core")
    placed = (P(ALL, None), P(ALL, None), P(), P(dp, None), P(dp))
    return jax.shard_map(
        shards, mesh=chips, in_specs=placed, out_specs=P(dp, None, "x", None), check_vma=False
    )
```

```python
import math

import jax
import jax.numpy as jnp
from jax import lax
from jax.experimental import pallas as pl
from jax.experimental.pallas import tpu as pltpu
from jax.sharding import Mesh
from jax.sharding import PartitionSpec as P

NSHARD = 8
T = 128
TOP_PRECISION = lax.Precision.HIGHEST
GRID = ("y", "z")
ALL = ("y", "z", "core", "x")


def dot(a, b, over_a, over_b):
    return lax.dot_general(
        a,
        b,
        (((over_a,), (over_b,)), ((), ())),
        precision=TOP_PRECISION,
        preferred_element_type=jnp.float32,
    )


def parts_of(v):
    high = v.astype(jnp.bfloat16)
    rest = v - high.astype(jnp.float32)
    middle = rest.astype(jnp.bfloat16)
    return high, middle, (rest - middle.astype(jnp.float32)).astype(jnp.bfloat16)


def long_dot(a, b, over_a, over_b):
    a1, a2, a3 = parts_of(a)
    b1, b2, b3 = parts_of(b)
    return lax.dot_general(
        jnp.concatenate([a1, a2, a1, a2, a1, a3], axis=over_a),
        jnp.concatenate([b1, b1, b2, b2, b3, b1], axis=over_b),
        (((over_a,), (over_b,)), ((), ())),
        preferred_element_type=jnp.float32,
    )


def place(n, i, j):
    return (i * n - i * (i - 1) // 2 + j - i) * T


def gram_kernel(core_ref, mine_ref, other_ref, g_ref, rows):
    n = mine_ref.shape[1] // T
    half = g_ref.shape[0] // T
    count = mine_ref.shape[0]
    rows[:count, :] = mine_ref[...]
    rows[count:, :] = other_ref[...]
    for side in range(2):

        @pl.when(core_ref[0] == side)
        def _(side=side):
            for i in range(n):
                first = place(n, i, i) // T
                low, high = max(first, side * half), min(first + n - i, (side + 1) * half)
                if low < high:
                    left = rows[:, i * T : (i + 1) * T]
                    right = rows[:, (i + low - first) * T : (i + high - first) * T]
                    product = dot(left, right, 0, 0)
                    for t in range(high - low):
                        at = pl.ds((low + t - side * half) * T, T)
                        g_ref[at, :] = product[:, t * T : (t + 1) * T]


def spread(row):
    return jnp.broadcast_to(row, (8, T))


def factor_block(rows, lane, sub, give):
    rows = list(rows)
    count = len(rows)
    for b in range(count):
        base = 8 * b
        columns = [spread(rows[b][:, base + j : base + j + 1]) for j in range(8)]
        inside = (lane >= base) & (lane < base + 8)
        work = jnp.where(inside, (lane - base == sub).astype(jnp.float32), rows[b])
        lower = jnp.where(lane < base + 8, work, 0.0)
        for j in range(8):
            inverse = 1.0 / columns[j][j : j + 1, :]
            pivot = sub == j
            row = spread(work[j : j + 1, :] * inverse)
            work = jnp.where(pivot, row, work - columns[j] * row)
            for l in range(j + 1, 8):
                entry = spread(columns[l][j : j + 1, :] * inverse)
                columns[l] = jnp.where(pivot, entry, columns[l] - columns[j] * entry)
        give(b, lower, jnp.where(lane < base + 8, work, 0.0))
        pivots = [spread(work[j : j + 1, :]) for j in range(8)]
        for i in range(b + 1, count):
            terms = [spread(rows[i][:, base + j : base + j + 1]) * pivots[j] for j in range(8)]
            while len(terms) > 1:
                terms = [terms[p] + terms[p + 1] for p in range(0, len(terms), 2)]
            rows[i] = jnp.where(inside, 0.0, rows[i]) - terms[0]
        yield b


def solve_kernel(total_rows, ridge_ref, core_ref, mine_ref, other_ref, f_ref, y_ref, a, x, pb, nm):
    n = f_ref.shape[1] // T
    half = mine_ref.shape[0]
    lane = lax.broadcasted_iota(jnp.int32, (8, T), 1)
    sub = lax.broadcasted_iota(jnp.int32, (8, T), 0)
    ridge = ridge_ref[0].astype(jnp.float32) / 16.0
    core = core_ref[0]
    a[pl.ds(pl.multiple_of(core * half, T), half), :] = mine_ref[...] * (1.0 / total_rows)
    a[pl.ds(pl.multiple_of((1 - core) * half, T), half), :] = other_ref[...] * (1.0 / total_rows)
    x[...] = f_ref[...]

    def block(i, j):
        return pl.ds(place(n, i, j), T)

    def panel(k, j):
        both = long_dot(nm[pl.ds(k * 2 * T, 2 * T), :], a[block(k, j), :], 1, 0)
        a[block(k, j), :] = both[:T]
        pb[block(k, j), :] = both[T:]

    def update(k, i, j):
        a[block(i, j), :] -= long_dot(a[block(k, i), :], pb[block(k, j), :], 0, 0)

    def forward(k):
        both = long_dot(x[:, k * T : (k + 1) * T], nm[pl.ds(k * 2 * T, 2 * T), :], 1, 1)
        x[:, k * T : (k + 1) * T] = both[:, :T]
        y_ref[:, k * T : (k + 1) * T] = both[:, T:]

    def forward_update(k, i):
        x[:, i * T : (i + 1) * T] -= long_dot(x[:, k * T : (k + 1) * T], pb[block(k, i), :], 1, 0)

    waiting = []
    for k in range(n):
        start = place(n, k, k)
        rows = [
            a[pl.ds(start + 8 * i, 8), :] + jnp.where(lane - 8 * i == sub, ridge, 0.0)
            for i in range(T // 8)
        ]

        def give(b, lower, scaled):
            nm[pl.ds(k * 2 * T + 8 * b, 8), :] = lower
            nm[pl.ds(k * 2 * T + T + 8 * b, 8), :] = scaled

        total, done = len(waiting), 0
        for b in factor_block(rows, lane, sub, give):
            while waiting and done < -(-total * (b + 1) // 14):
                step, *where = waiting.pop(0)
                step(*where)
                done += 1
        if k + 1 < n:
            panel(k, k + 1)
            update(k, k + 1, k + 1)
            waiting = [(panel, k, j) for j in range(k + 2, n)] + [(forward, k)]
            for i in range(k + 1, n):
                waiting += [(update, k, i, j) for j in range(i, n) if j > k + 1]
                waiting += [(forward_update, k, i)]
    forward(n - 1)
    for k in reversed(range(n)):
        yk = long_dot(y_ref[:, k * T : (k + 1) * T], nm[pl.ds(k * 2 * T, T), :], 1, 0)
        y_ref[:, k * T : (k + 1) * T] = yk
        for i in reversed(range(k)):
            y_ref[:, i * T : (i + 1) * T] -= long_dot(yk, pb[block(i, k), :], 1, 1)


def scores_kernel(scale, q_ref, y_ref, table_ref):
    pieces = y_ref.shape[1] // T
    count = table_ref.shape[0]
    total = jnp.zeros(table_ref.shape, jnp.float32)
    for s in range(pieces):
        total += long_dot(q_ref[pl.ds(s, count, stride=pieces), :], y_ref[:, s * T : (s + 1) * T], 1, 1)
    table_ref[...] = total * scale


def pick_kernel(listing_ref, count_ref, got_ref, out_ref):
    group = got_ref.shape[1]
    for l in range(NSHARD):
        live = l < count_ref[0]
        shard = listing_ref[0, l]
        for g in range(group):
            tile = jnp.where(live, got_ref[shard, g], 0.0)
            for q in range(got_ref.shape[2]):
                out_ref[q, l, :, g * T : (g + 1) * T] = tile[q : q + 1]


def shards(features, queries, ridge_sixteenths, shard_lists, counts):
    width = features.shape[1]
    n = width // T
    n_y, n_z, n_x = lax.axis_size("y"), lax.axis_size("z"), lax.axis_size("x")
    n_grid = n_y * n_z
    total_rows = features.shape[0] * n_grid * 2 * n_x
    packed = n * (n + 1) // 2 * T
    half = packed // 2
    piece = half // n_x
    chunk = piece * T // n_grid
    core = lax.axis_index("core")
    vmem = pl.BlockSpec(memory_space=pltpu.VMEM)
    smem = pl.BlockSpec(memory_space=pltpu.SMEM)
    swap = [(0, 1), (1, 0)]

    all_queries = lax.all_gather(queries.reshape(n, T), ALL, axis=0, tiled=True)
    core_here = core.reshape(1).astype(jnp.int32)
    with jax.named_scope("gram"):
        neighbour = lax.ppermute(features, "core", swap)
        part = pl.pallas_call(
            gram_kernel,
            out_shape=jax.ShapeDtypeStruct((half, T), jnp.float32),
            in_specs=[smem, vmem, vmem],
            out_specs=vmem,
            scratch_shapes=[pltpu.VMEM((2 * features.shape[0], width), jnp.float32)],
            compiler_params=pltpu.CompilerParams(vmem_limit_bytes=32 * 1024 * 1024),
        )(core_here, features, neighbour)
    with jax.named_scope("scatter"):
        part = lax.all_to_all(part.reshape(n_x, piece, T), "x", 0, 0, tiled=True).sum(0)
        part = lax.all_to_all(part.reshape(n_grid, chunk), GRID, 0, 0, tiled=True).sum(0)
    with jax.named_scope("gather"):
        part = lax.all_to_all(jnp.broadcast_to(part[None], (n_grid, chunk)), GRID, 0, 0, tiled=True)
        part = jnp.broadcast_to(part.reshape(1, piece, T), (n_x, piece, T))
        mine = lax.all_to_all(part, "x", 0, 0, tiled=True).reshape(half, T)
        other = lax.ppermute(mine, "core", swap)
    with jax.named_scope("solve"):
        solved = pl.pallas_call(
            lambda *refs: solve_kernel(total_rows, *refs),
            out_shape=jax.ShapeDtypeStruct(features.shape, jnp.float32),
            in_specs=[smem, smem, vmem, vmem, vmem],
            out_specs=vmem,
            scratch_shapes=[
                pltpu.VMEM((packed, T), jnp.float32),
                pltpu.VMEM(features.shape, jnp.float32),
                pltpu.VMEM((packed, T), jnp.float32),
                pltpu.VMEM((2 * width, T), jnp.float32),
            ],
            compiler_params=pltpu.CompilerParams(vmem_limit_bytes=40 * 1024 * 1024),
        )(ridge_sixteenths, core_here, mine, other, features)
    with jax.named_scope("scores"):
        table = pl.pallas_call(
            lambda *refs: scores_kernel(1.0 / math.sqrt(width), *refs),
            out_shape=jax.ShapeDtypeStruct((all_queries.shape[0] // n, T), jnp.float32),
            in_specs=[vmem, vmem],
            out_specs=vmem,
            compiler_params=pltpu.CompilerParams(vmem_limit_bytes=32 * 1024 * 1024),
        )(all_queries, solved)
    n_dp = n_grid * 2
    block = table.shape[0] // n_dp
    group = n_dp // NSHARD
    got = lax.all_to_all(table.reshape(n_dp, block, T), ("y", "z", "core"), 0, 0, tiled=True)
    with jax.named_scope("pick"):
        picked = pl.pallas_call(
            pick_kernel,
            out_shape=jax.ShapeDtypeStruct((block, NSHARD, 1, group * T), jnp.float32),
            in_specs=[smem, smem, vmem],
            out_specs=vmem,
        )(shard_lists, counts, got.reshape(NSHARD, group, block, T))
    return picked


def solution(mesh):
    n_dp, n_x = mesh.devices.shape
    side = math.isqrt(n_dp // 2)
    chips = Mesh(mesh.devices.reshape(side, side, 2, n_x), ALL)
    dp = ("y", "z", "core")
    placed = (P(ALL, None), P(ALL, None), P(), P(dp, None), P(dp))
    return jax.shard_map(
        shards, mesh=chips, in_specs=placed, out_specs=P(dp, None, "x", None), check_vma=False
    )
```
